512 devices in a mesh: tri: 64 (over y, z), sub: 8 (over x, core).
Axes of the slice: x: 4, y: 4, z: 16, core: 2. Of those that a mesh axis runs over, the one named last changes fastest.
Arguments:
- stored_tiles: float32 [64, 10, 512, 512], P('tri', None, 'sub'), may hold values from -190 to 190, as said below
- cell_owner: int32 [64], replicated, may hold values from 0 to 63, as said below
Outputs:
- updated: float32 [64, 10, 512, 512], P('tri', None, 'sub')
The draws below stay inside these ranges and needn't reach their ends.
Inputs may be any that keep to these rules, and one draw needn't show every extreme that they name: `cell_owner`: a permutation of the indices of tri. `stored_tiles`: every tile whose row and column blocks are equal is skew-symmetric, every pivot met is invertible, and slots that hold no tile are zero.
All inputs are finite; a program needn't handle non-finite values.
Results may differ from the reference program's by a relative error of at most 0.00035.
Values may be sent and summed in bfloat16 or wider, within the bound.
A program may use at most 64 MiB of HBM per device.

```python
import math
import jax
import jax.numpy as jnp
import numpy as np
from jax import lax

NB = 32
BS = 512
STEPS = 1
N_TRI = 64


def layout_drawn(groups, per_group):
    half_group = per_group // 2
    slot_count = per_group * (per_group + 1) // 2
    row_table = np.full((groups * groups, slot_count), -1, np.int32)
    col_table = np.full((groups * groups, slot_count), -1, np.int32)
    for first_group in range(groups):
        for second_group in range(groups):
            cell_index = first_group * groups + second_group
            for inner_row in range(per_group):
                if first_group == second_group:
                    for inner_column in range(inner_row + 1):
                        slot_index = inner_row * (inner_row + 1) // 2 + inner_column
                        row_table[cell_index, slot_index] = first_group * per_group + inner_row
                        col_table[cell_index, slot_index] = first_group * per_group + inner_column
                else:
                    for inner_column in range(half_group):
                        slot_index = inner_row * half_group + inner_column
                        if first_group > second_group:
                            row_table[cell_index, slot_index] = first_group * per_group + inner_row
                            col_table[cell_index, slot_index] = second_group * per_group + inner_column
                        else:
                            row_table[cell_index, slot_index] = second_group * per_group + inner_row
                            col_table[cell_index, slot_index] = first_group * per_group + half_group + inner_column
    return (row_table, col_table)


def cell_draw(key):
    return jax.random.permutation(jax.random.fold_in(key, 11), N_TRI).astype(jnp.int32)


def draw_cell_owner(key, part):
    return cell_draw(key)


def draw_stored_tiles(key, part):
    owners = cell_draw(key)
    cell_of = jnp.zeros((N_TRI,), jnp.int32).at[owners].set(jnp.arange(N_TRI, dtype=jnp.int32))
    groups = math.isqrt(N_TRI)
    per_group = NB // groups
    row_table, col_table = layout_drawn(groups, per_group)
    row_ids = jnp.asarray(row_table)[cell_of]
    col_ids = jnp.asarray(col_table)[cell_of]
    slot_count = row_table.shape[1]
    tile_shape = (N_TRI, slot_count, BS, BS)
    first_key = jax.random.fold_in(key, 1)
    second_key = jax.random.fold_in(key, 2)
    noise_draw = jnp.clip(jax.random.normal(first_key, tile_shape, jnp.float32), -4.0, 4.0)
    skew_part = 1.2 * (noise_draw - jnp.swapaxes(noise_draw, 2, 3)) / math.sqrt(2.0)
    pair_values = 90.0 * jnp.exp(jax.random.uniform(second_key, (N_TRI, slot_count, BS // 2), jnp.float32, 0.0, math.log(2.0)))
    spread_values = jnp.repeat(pair_values, 2, axis=2)
    row_index = jnp.arange(BS)
    partner_index = row_index + 1 - 2 * (row_index % 2)
    sign_of_row = (1 - 2 * (row_index % 2)).astype(jnp.float32)
    pair_mask = row_index[None, :] == partner_index[:, None]
    pair_part = jnp.where(pair_mask, sign_of_row[:, None] * spread_values[..., :, None], 0.0)
    diagonal = (row_ids == col_ids) & (row_ids >= 0)
    empty_slot = row_ids < 0
    drawn_part = jnp.where(empty_slot[..., None, None], 0.0, 0.5 * noise_draw)
    return jnp.where(diagonal[..., None, None], skew_part + pair_part, drawn_part)


def setup_inputs(seed: int = 0) -> dict:
    key_list = jax.random.split(jax.random.key(seed), 3)
    return {
        "stored_tiles": draw_stored_tiles(jax.random.fold_in(key_list[2], 71), 0),
        "cell_owner": draw_cell_owner(jax.random.fold_in(key_list[2], 71), 0),
    }


def layout(groups, per_group):
    half_group = per_group // 2
    slot_count = per_group * (per_group + 1) // 2
    row_table = np.full((groups * groups, slot_count), -1, np.int32)
    col_table = np.full((groups * groups, slot_count), -1, np.int32)
    for first_group in range(groups):
        for second_group in range(groups):
            cell_index = first_group * groups + second_group
            for inner_row in range(per_group):
                if first_group == second_group:
                    for inner_column in range(inner_row + 1):
                        slot_index = inner_row * (inner_row + 1) // 2 + inner_column
                        row_table[cell_index, slot_index] = first_group * per_group + inner_row
                        col_table[cell_index, slot_index] = first_group * per_group + inner_column
                else:
                    for inner_column in range(half_group):
                        slot_index = inner_row * half_group + inner_column
                        if first_group > second_group:
                            row_table[cell_index, slot_index] = first_group * per_group + inner_row
                            col_table[cell_index, slot_index] = second_group * per_group + inner_column
                        else:
                            row_table[cell_index, slot_index] = second_group * per_group + inner_row
                            col_table[cell_index, slot_index] = first_group * per_group + half_group + inner_column
    return (row_table, col_table)

def reference(stored_tiles, cell_owner):
    groups = math.isqrt(N_TRI)
    per_group = NB // groups
    row_table, col_table = layout(groups, per_group)
    locate = {}
    for cell_index in range(row_table.shape[0]):
        for slot_index in range(row_table.shape[1]):
            if row_table[cell_index, slot_index] >= 0:
                locate[int(row_table[cell_index, slot_index]), int(col_table[cell_index, slot_index])] = (cell_index, slot_index)
    highest = lax.Precision.HIGHEST
    by_cell = stored_tiles[cell_owner]
    row_ids = jnp.asarray(row_table)
    col_ids = jnp.asarray(col_table)
    for step_index in range(STEPS):
        source_cells = np.array([locate[member, step_index][0] for member in range(step_index + 1, NB)], np.int32)
        source_slots = np.array([locate[member, step_index][1] for member in range(step_index + 1, NB)], np.int32)
        column_tiles = by_cell[source_cells, source_slots].astype(jnp.bfloat16)
        pivot_cell, pivot_slot = locate[step_index, step_index]
        pivot_block = by_cell[pivot_cell, pivot_slot]
        inverse = jnp.linalg.inv(pivot_block)
        padded = jnp.concatenate([jnp.zeros((step_index + 1, BS, BS), jnp.bfloat16), column_tiles], axis=0)
        scaled = jnp.einsum('nrk,kc->nrc', padded.astype(jnp.float32), inverse, precision=highest).astype(jnp.bfloat16)

        def cell_update(operands):
            cell_tiles, cell_rows, cell_cols = operands
            live_slots = (cell_rows > step_index) & (cell_cols > step_index)
            left_side = scaled[jnp.maximum(cell_rows, 0)].astype(jnp.float32)
            right_side = padded[jnp.maximum(cell_cols, 0)].astype(jnp.float32)
            product = jnp.einsum('qrk,qck->qrc', left_side, right_side, precision=highest)
            return cell_tiles + jnp.where(live_slots[:, None, None], product, 0.0)
        by_cell = lax.map(cell_update, (by_cell, row_ids, col_ids))
    return jnp.zeros_like(stored_tiles).at[cell_owner].set(by_cell)
```

```python
import functools

import jax
import jax.numpy as jnp
from jax import lax
from jax.experimental import pallas as pl
from jax.experimental.pallas import tpu as pltpu
from jax.sharding import Mesh
from jax.sharding import PartitionSpec as P

MESH = pl.DeviceIdType.MESH
AXES = ("y", "z", "x", "c")
NY, NZ, NX, NC = 4, 16, 4, 2
TRI = NY * NZ
SUB = NX * NC
GROUPS = 8
PER = 4
N = 512
ROWS = N // SUB
LANES = 128
CB = N // LANES
PIECE = 16
LOAD_SLOTS = (0, 1, 2, 3, 4, 6)
FIRST_SLOTS = (0, 1, 3, 6)
NEWTON_STEPS = 6
NEWTON_LOW = 0.004
BF = jnp.bfloat16
F32 = jnp.float32


def drain(ref, sem):
    pltpu.make_async_copy(ref, ref, sem).wait()


def send(src, dst, send_sem, recv_sem, device):
    pltpu.make_async_remote_copy(
        src_ref=src,
        dst_ref=dst,
        send_sem=send_sem,
        recv_sem=recv_sem,
        device_id=device,
        device_id_type=MESH,
    ).start()


def cells_at(owner_ref, places):
    def body(c, found):
        owner = owner_ref[c]
        return tuple(jnp.where(owner == t, c, f) for t, f in zip(places, found))

    zero = jnp.int32(0)
    return lax.fori_loop(0, TRI, body, tuple(zero for _ in places))


def groups_of(cell):
    down = lax.shift_right_logical(cell, jnp.int32(3))
    across = lax.bitwise_and(cell, jnp.int32(7))
    first = jnp.where(down < across, 2, 0)
    return jnp.maximum(down, across), jnp.minimum(down, across), first


def route_kernel(
    owner_ref,
    tiles_ref,
    fin,
    right,
    piv,
    loaded,
    panel,
    a2r,
    yb,
    msg,
    pyr,
    psel,
    wz,
    mz,
    load_sem,
    p_send,
    p_recv,
    a_send,
    a_recv,
    m_send,
    m_recv,
    y_send,
    y_recv,
    w_send,
    w_recv,
    x_send,
    x_recv,
    c_send,
    c_recv,
    q_send,
    q_recv,
):
    y, z = lax.axis_index("y"), lax.axis_index("z")
    x, c = lax.axis_index("x"), lax.axis_index("c")
    me = y * NZ + z
    u = x * NC + c
    res = lax.rem(z, 4)
    quo = z // 4
    far2 = 2 + 12 * c
    window = (1, 15, far2)
    mates = (4, 12, 8)
    others4 = (1, 3, 2)

    for k, slot in enumerate(LOAD_SLOTS):
        pltpu.make_async_copy(tiles_ref.at[0, slot], loaded.at[k], load_sem).start()

    barrier = pltpu.get_barrier_semaphore()

    def greet(k, carry):
        ty, tz = lax.rem(y + k // NZ, NY), lax.rem(z + lax.rem(k, NZ), NZ)
        pl.semaphore_signal(barrier, inc=1, device_id=(ty, tz, x, c), device_id_type=MESH)
        return carry

    lax.fori_loop(1, TRI, greet, 0)
    for dx in others4:
        pl.semaphore_signal(
            barrier, inc=1, device_id=(y, z, lax.rem(x + dx, NX), c), device_id_type=MESH
        )
    pl.semaphore_signal(barrier, inc=1, device_id=(y, z, x, 1 - c), device_id_type=MESH)

    tri_of = lambda dz: y * NZ + lax.rem(z + dz, NZ)
    cells = cells_at(owner_ref, (me, tri_of(1), tri_of(15), tri_of(far2)))
    pivot_at = owner_ref[0]
    y0 = lax.shift_right_logical(pivot_at, jnp.int32(4))
    z0 = lax.bitwise_and(pivot_at, jnp.int32(15))

    drain(loaded, load_sem)
    is_first = cells[0] < GROUPS
    for i in range(PER):
        low = loaded[LOAD_SLOTS.index(2 * i)]
        top = loaded[LOAD_SLOTS.index(FIRST_SLOTS[i])]
        tile = jnp.where(is_first, top, low).astype(BF)
        for b in range(CB):
            panel[i, b] = tile[:, b * LANES : (b + 1) * LANES]
    pl.semaphore_wait(barrier, TRI - 1 + 4)

    def spread(lo, hi):
        def body(k, carry):
            ty, tz = lax.rem(y + k // NZ, NY), lax.rem(z + lax.rem(k, NZ), NZ)
            row = pl.multiple_of((tz // 4) * PIECE, PIECE)
            send(
                panel.at[ty, lax.rem(tz, 4), pl.ds(row, PIECE)],
                a2r.at[me],
                a_send,
                a_recv,
                (ty, tz, x, c),
            )
            return carry

        lax.fori_loop(lo, hi, body, 0)

    my_row = pl.multiple_of(quo * PIECE, PIECE)
    res_row = pl.multiple_of(res * PIECE, PIECE)

    for k, dy in enumerate(others4):
        ty = lax.rem(y + dy, NY)
        send(panel.at[0, ty], pyr.at[y], p_send.at[0], p_recv.at[0], (ty, z, x, c))
    pyr[y] = panel[0, y]
    spread(1, 16)
    drain(pyr.at[0:3], p_recv.at[0])
    psel[...] = pyr[y0]
    for k, dz in enumerate(window):
        tz = lax.rem(z + dz, NZ)
        row = pl.multiple_of(lax.rem(tz, 4) * PIECE, PIECE)
        send(
            psel.at[pl.ds(row, PIECE)], wz.at[k + 1], p_send.at[1], p_recv.at[1], (y, tz, x, c)
        )
    wz[0] = psel[pl.ds(res_row, PIECE)]
    spread(16, 32)
    drain(wz.at[0:3], p_recv.at[1])
    delta = lax.bitwise_and(z - z0, 15)
    came = jnp.where(delta == 1, 1, jnp.where(delta == 15, 2, jnp.where(delta == far2, 3, 0)))
    mz[0] = wz[came]
    for k, dz in enumerate(mates):
        send(
            mz.at[0],
            mz.at[k + 1],
            p_send.at[2],
            p_recv.at[2],
            (y, lax.rem(z + dz, NZ), x, c),
        )
    spread(32, 48)
    drain(mz.at[1:4], p_recv.at[2])
    came = jnp.int32(0)
    for k, dz in enumerate(mates):
        delta = lax.bitwise_and(z - dz - z0, 15)
        valid = (delta == 0) | (delta == 1) | (delta == 15) | (delta == far2)
        came = jnp.where(valid, k + 1, came)
    part = piv.at[u, y]
    part[pl.ds(res_row, PIECE)] = mz[came]
    for k, dz in enumerate(window):
        send(
            part.at[pl.ds(res_row, PIECE)],
            part.at[pl.ds(res_row, PIECE)],
            p_send.at[3],
            p_recv.at[3],
            (y, lax.rem(z + dz, NZ), x, c),
        )
    spread(48, 64)
    drain(mz.at[1:4], p_recv.at[3])
    for k, dy in enumerate(others4):
        send(part, part, p_send.at[4], p_recv.at[4], (lax.rem(y + dy, NY), z, x, c))
    drain(pyr.at[0:3], p_recv.at[4])
    strip = piv.at[u]
    for k, dx in enumerate(others4):
        send(strip, strip, p_send.at[5], q_recv.at[k], (y, z, lax.rem(x + dx, NX), c))
    send(strip, strip, q_send, p_recv.at[5], (y, z, x, 1 - c))

    a2r[me] = panel[y, res, pl.ds(my_row, PIECE)]
    drain(a2r.at[0 : TRI - 1], a_recv)
    gathered = yb.at[y]
    for g in range(GROUPS):
        gathered[g, pl.ds(my_row, PIECE)] = a2r[owner_ref[g * GROUPS]]
    for k, dz in enumerate(mates):
        piece = gathered.at[:, pl.ds(my_row, PIECE)]
        send(piece, piece, m_send, m_recv, (y, lax.rem(z + dz, NZ), x, c))

    for k, dx in enumerate(others4):
        drain(strip, q_recv.at[k])
        source = lax.rem(x - dx + NX, NX) * NC + c
        send(piv.at[source], piv.at[source], q_send, p_recv.at[5], (y, z, x, 1 - c))

    drain(gathered.at[:, 0 : 3 * PIECE], m_recv)
    for k, dy in enumerate(others4):
        send(gathered, gathered, y_send, y_recv, (lax.rem(y + dy, NY), z, x, c))
    drain(yb.at[0:3], y_recv)

    def pick(cell, out):
        row_group, col_group, first = groups_of(cell)
        for i in range(PER):
            out[i] = yb[i, row_group]
        for j in range(2):
            out[PER + j] = yb[first + j, col_group]

    for k, dz in enumerate(window):
        pick(cells[k + 1], msg.at[k])
        send(
            msg.at[k], fin.at[res], w_send, w_recv.at[k], (y, lax.rem(z + dz, NZ), x, c)
        )
    pick(cells[0], fin.at[res])

    for part_no in range(4):
        if part_no > 0:
            drain(msg.at[0], w_recv.at[part_no - 1])
        b = lax.rem(z - (0, 1, 15, far2)[part_no] + NZ, 4)
        right[u, b] = fin[b, 2:6]
        for k, dx in enumerate(others4):
            send(
                fin.at[b, 2:6],
                right.at[u, b],
                x_send,
                x_recv.at[part_no, k],
                (y, z, lax.rem(x + dx, NX), c),
            )
        send(fin.at[b, 2:6], right.at[u, b], c_send, c_recv, (y, z, x, 1 - c))
    for part_no in range(4):
        b = lax.rem(z - (0, 1, 15, far2)[part_no] + NZ, 4)
        for k, dx in enumerate(others4):
            drain(right.at[0, 0], x_recv.at[part_no, k])
            source = lax.rem(x - dx + NX, NX) * NC + c
            send(right.at[source, b], right.at[source, b], c_send, c_recv, (y, z, x, 1 - c))
    drain(right.at[0:4], c_recv)
    drain(piv.at[0:4], p_recv.at[5])

    drain(pyr.at[0:3], p_send.at[0])
    drain(wz.at[0:3], p_send.at[1])
    drain(mz.at[1:4], p_send.at[2])
    drain(mz.at[1:4], p_send.at[3])
    drain(pyr.at[0:3], p_send.at[4])
    drain(piv.at[0:3], p_send.at[5])
    drain(piv.at[0:4], q_send)
    drain(a2r.at[0 : TRI - 1], a_send)
    drain(gathered.at[:, 0 : 3 * PIECE], m_send)
    drain(yb.at[0:3], y_send)
    drain(msg, w_send)
    drain(right.at[0:3], x_send)
    drain(right.at[0:4], c_send)


def dot(a, b, precision=None):
    return lax.dot_general(
        a, b, (((1,), (0,)), ((), ())), precision=precision, preferred_element_type=F32
    )


def dot_nt(a, b):
    return lax.dot_general(a, b, (((1,), (1,)), ((), ())), preferred_element_type=F32)


def schedule(low, steps):
    out, scale = [], 1.0
    for _ in range(steps):
        s = (1 + low) / (1 - low)
        t = 2 * s * s - 1
        out.append((8 * (1 + low) / (1 - low) ** 2 / t / scale, 8 / (1 - low) ** 2 / t / scale**2))
        scale, low = 1 + 1 / t, (1 - 1 / t) / (1 + 1 / t)
    return out


def identity():
    shape = (N, N)
    return lax.broadcasted_iota(jnp.int32, shape, 0) == lax.broadcasted_iota(jnp.int32, shape, 1)


def newton(p, xb, yv):
    yv[...] = dot_nt(p[...], p[...])
    bound = jnp.max(jnp.sum(jnp.abs(yv[...]), axis=0, keepdims=True))
    inv = 1.0 / bound
    xb[...] = (p[...].astype(F32) * -inv).astype(BF)
    yv[...] = yv[...] * inv
    coefs = schedule(NEWTON_LOW, NEWTON_STEPS)

    def step(k, carry):
        c1, c2 = jnp.float32(coefs[0][0]), jnp.float32(coefs[0][1])
        for i in range(1, NEWTON_STEPS):
            c1 = jnp.where(k == i, coefs[i][0], c1)
            c2 = jnp.where(k == i, coefs[i][1], c2)
        m = (jnp.where(identity(), c1, 0.0) - c2 * yv[...]).astype(BF)
        xb[...] = dot(xb[...], m).astype(BF)
        yv[...] = dot(p[...], xb[...])
        return carry

    lax.fori_loop(0, NEWTON_STEPS, step, 0)


def update_kernel(
    owner_ref, tiles_ref, fin, right, piv, out_ref, cur, p, xb, xf, yv, rt, left, in_sem, out_sem
):
    for slot in range(10):
        pltpu.make_async_copy(tiles_ref.at[0, slot], cur.at[slot], in_sem.at[slot]).start()
    me = lax.axis_index("y") * NZ + lax.axis_index("z")
    (cell,) = cells_at(owner_ref, (me,))
    row_group, col_group, first = groups_of(cell)
    diagonal = row_group == col_group

    for v in range(SUB):
        for b in range(CB):
            p[v * ROWS : (v + 1) * ROWS, b * LANES : (b + 1) * LANES] = piv[v, b]
    newton(p, xb, yv)

    yv[...] = jnp.where(identity(), 1.0, 0.0) - yv[...]
    xf[...] = xb[...].astype(F32)
    highest = lax.Precision.HIGHEST
    size = jnp.sum(yv[...] * yv[...])

    @pl.when(jnp.logical_not(size < 0.01))
    def _():
        @pl.when(jnp.logical_not(size < 0.25))
        def _():
            whole = p[...].astype(F32)
            rows = jnp.max(jnp.sum(jnp.abs(whole), axis=0, keepdims=True))
            xf[...] = whole * (-1.0 / rows) / rows

        def residual():
            yv[...] = jnp.where(identity(), 1.0, 0.0) - dot(
                p[...].astype(F32), xf[...], highest
            )
            return jnp.sum(yv[...] * yv[...])

        def more(carry):
            k, size = carry
            xf[...] = xf[...] + dot(xf[...], yv[...], highest)
            return k + 1, residual()

        lax.while_loop(lambda s: (s[0] < 150) & (s[1] > 0.001), more, (0, residual()))

    small = yv[...].astype(BF)
    yv[...] = yv[...] + dot(small, small)
    xf[...] = xf[...] + dot(xf[...].astype(BF), yv[...].astype(BF))

    high = xf[...].astype(BF)
    xb[...] = high
    xf[...] = xf[...] - high.astype(F32)
    for i in range(PER):
        strip = jnp.concatenate([fin[b, i] for b in range(CB)], axis=1)
        left[i * ROWS : (i + 1) * ROWS] = (
            dot(strip, xb[...]) + dot(strip, xf[...].astype(BF))
        ).astype(BF)

    def stage(j, strip):
        for v in range(SUB):
            for b in range(CB):
                rt[j, v * ROWS : (v + 1) * ROWS, b * LANES : (b + 1) * LANES] = right[v, b, strip]

    for slot in range(10):
        pltpu.make_async_copy(tiles_ref.at[0, slot], cur.at[slot], in_sem.at[slot]).wait()
    stage(0, 2)
    stage(1, 3)

    @pl.when(diagonal)
    def _():
        stage(2, 0)
        stage(3, 1)
        for j in range(PER):
            live = (row_group > 0) | (j > 0)
            product = dot_nt(left[j * ROWS :], rt[j])
            for i in range(j, PER):
                slot = i * (i + 1) // 2 + j
                term = product[(i - j) * ROWS : (i - j + 1) * ROWS]
                cur[slot] = cur[slot] + jnp.where(live, term, 0.0)

    @pl.when(jnp.logical_not(diagonal))
    def _():
        for j in range(2):
            live = col_group * PER + first + j > 0
            product = dot_nt(left[...], rt[j])
            for i in range(PER):
                slot = 2 * i + j
                term = product[i * ROWS : (i + 1) * ROWS]
                cur[slot] = cur[slot] + jnp.where(live, term, 0.0)

    for slot in range(10):
        pltpu.make_async_copy(cur.at[slot], out_ref.at[0, slot], out_sem.at[slot]).start()
    for slot in range(10):
        pltpu.make_async_copy(cur.at[slot], out_ref.at[0, slot], out_sem.at[slot]).wait()


def shards(stored_tiles, cell_owner):
    dma = pltpu.SemaphoreType.DMA
    vmem = pl.BlockSpec(memory_space=pltpu.VMEM)
    smem = pl.BlockSpec(memory_space=pltpu.SMEM)
    hbm = pl.BlockSpec(memory_space=pl.ANY)
    strip = (ROWS, LANES)
    fin, right, piv = pl.pallas_call(
        route_kernel,
        out_shape=(
            jax.ShapeDtypeStruct((CB, 6, *strip), BF),
            jax.ShapeDtypeStruct((SUB, CB, 4, *strip), BF),
            jax.ShapeDtypeStruct((SUB, CB, *strip), BF),
        ),
        in_specs=[smem, hbm],
        out_specs=(vmem, vmem, vmem),
        scratch_shapes=[
            pltpu.VMEM((len(LOAD_SLOTS), ROWS, N), F32),
            pltpu.VMEM((PER, CB, *strip), BF),
            pltpu.VMEM((TRI, PIECE, LANES), BF),
            pltpu.VMEM((PER, GROUPS, *strip), BF),
            pltpu.VMEM((3, 6, *strip), BF),
            pltpu.VMEM((NY, *strip), BF),
            pltpu.VMEM(strip, BF),
            pltpu.VMEM((4, PIECE, LANES), BF),
            pltpu.VMEM((4, PIECE, LANES), BF),
            dma,
            dma((6,)),
            dma((6,)),
            dma,
            dma,
            dma,
            dma,
            dma,
            dma,
            dma,
            dma((3,)),
            dma,
            dma((4, 3)),
            dma,
            dma,
            dma,
            dma((3,)),
        ],
        compiler_params=pltpu.CompilerParams(
            collective_id=0, has_side_effects=True, vmem_limit_bytes=40 * 2**20
        ),
    )(cell_owner, stored_tiles)
    return pl.pallas_call(
        update_kernel,
        out_shape=jax.ShapeDtypeStruct(stored_tiles.shape, F32),
        in_specs=[smem, hbm, vmem, vmem, vmem],
        out_specs=hbm,
        scratch_shapes=[
            pltpu.VMEM((10, ROWS, N), F32),
            pltpu.VMEM((N, N), BF),
            pltpu.VMEM((N, N), BF),
            pltpu.VMEM((N, N), F32),
            pltpu.VMEM((N, N), F32),
            pltpu.VMEM((PER, N, N), BF),
            pltpu.VMEM((PER * ROWS, N), BF),
            dma((10,)),
            dma((10,)),
        ],
        compiler_params=pltpu.CompilerParams(vmem_limit_bytes=40 * 2**20),
    )(cell_owner, stored_tiles, fin, right, piv)


def solution(mesh):
    torus = Mesh(mesh.devices.reshape(NY, NZ, NX, NC), AXES)
    spec = P(("y", "z"), None, ("x", "c"), None)
    return jax.shard_map(
        shards, mesh=torus, in_specs=(spec, P()), out_specs=spec, check_vma=False
    )
```

```python
import functools

import jax
import jax.numpy as jnp
from jax import lax
from jax.experimental import pallas as pl
from jax.experimental.pallas import tpu as pltpu
from jax.sharding import Mesh
from jax.sharding import PartitionSpec as P

MESH = pl.DeviceIdType.MESH
AXES = ("y", "z", "x", "c")
NY, NZ, NX, NC = 4, 16, 4, 2
TRI = NY * NZ
SUB = NX * NC
GROUPS = 8
PER = 4
N = 512
ROWS = N // SUB
LANES = 128
CB = N // LANES
PIECE = 16
LOAD_SLOTS = (0, 1, 2, 3, 4, 6)
FIRST_SLOTS = (0, 1, 3, 6)
NEWTON_STEPS = 6
NEWTON_LOW = 0.004
BF = jnp.bfloat16
F32 = jnp.float32


def drain(ref, sem):
    pltpu.make_async_copy(ref, ref, sem).wait()


def send(src, dst, send_sem, recv_sem, device):
    pltpu.make_async_remote_copy(
        src_ref=src,
        dst_ref=dst,
        send_sem=send_sem,
        recv_sem=recv_sem,
        device_id=device,
        device_id_type=MESH,
    ).start()


def cells_at(owner_ref, places):
    def body(c, found):
        owner = owner_ref[c]
        return tuple(jnp.where(owner == t, c, f) for t, f in zip(places, found))

    zero = jnp.int32(0)
    return lax.fori_loop(0, TRI, body, tuple(zero for _ in places))


def groups_of(cell):
    down = lax.shift_right_logical(cell, jnp.int32(3))
    across = lax.bitwise_and(cell, jnp.int32(7))
    first = jnp.where(down < across, 2, 0)
    return jnp.maximum(down, across), jnp.minimum(down, across), first


def route_kernel(
    owner_ref,
    tiles_ref,
    fin,
    right,
    piv,
    xb,
    xl,
    size_ref,
    p,
    xf,
    yv,
    loaded,
    panel,
    a2r,
    yb,
    msg,
    pyr,
    psel,
    wz,
    mz,
    load_sem,
    p_send,
    p_recv,
    a_send,
    a_recv,
    m_send,
    m_recv,
    y_send,
    y_recv,
    w_send,
    w_recv,
    x_send,
    x_recv,
    c_send,
    c_recv,
    q_send,
    q_recv,
):
    y, z = lax.axis_index("y"), lax.axis_index("z")
    x, c = lax.axis_index("x"), lax.axis_index("c")
    me = y * NZ + z
    u = x * NC + c
    res = lax.rem(z, 4)
    quo = z // 4
    far2 = 2 + 12 * c
    window = (1, 15, far2)
    mates = (4, 12, 8)
    others4 = (1, 3, 2)

    for k, slot in enumerate(LOAD_SLOTS):
        pltpu.make_async_copy(tiles_ref.at[0, slot], loaded.at[k], load_sem).start()

    barrier = pltpu.get_barrier_semaphore()

    def greet(k, carry):
        ty, tz = lax.rem(y + k // NZ, NY), lax.rem(z + lax.rem(k, NZ), NZ)
        pl.semaphore_signal(barrier, inc=1, device_id=(ty, tz, x, c), device_id_type=MESH)
        return carry

    lax.fori_loop(1, TRI, greet, 0)
    for dx in others4:
        pl.semaphore_signal(
            barrier, inc=1, device_id=(y, z, lax.rem(x + dx, NX), c), device_id_type=MESH
        )
    pl.semaphore_signal(barrier, inc=1, device_id=(y, z, x, 1 - c), device_id_type=MESH)

    tri_of = lambda dz: y * NZ + lax.rem(z + dz, NZ)
    cells = cells_at(owner_ref, (me, tri_of(1), tri_of(15), tri_of(far2)))
    pivot_at = owner_ref[0]
    y0 = lax.shift_right_logical(pivot_at, jnp.int32(4))
    z0 = lax.bitwise_and(pivot_at, jnp.int32(15))

    drain(loaded, load_sem)
    is_first = cells[0] < GROUPS
    for i in range(PER):
        low = loaded[LOAD_SLOTS.index(2 * i)]
        top = loaded[LOAD_SLOTS.index(FIRST_SLOTS[i])]
        tile = jnp.where(is_first, top, low).astype(BF)
        for b in range(CB):
            panel[i, b] = tile[:, b * LANES : (b + 1) * LANES]
    pl.semaphore_wait(barrier, TRI - 1 + 4)

    def spread(lo, hi):
        def body(k, carry):
            ty, tz = lax.rem(y + k // NZ, NY), lax.rem(z + lax.rem(k, NZ), NZ)
            row = pl.multiple_of((tz // 4) * PIECE, PIECE)
            send(
                panel.at[ty, lax.rem(tz, 4), pl.ds(row, PIECE)],
                a2r.at[me],
                a_send,
                a_recv,
                (ty, tz, x, c),
            )
            return carry

        lax.fori_loop(lo, hi, body, 0)

    my_row = pl.multiple_of(quo * PIECE, PIECE)
    res_row = pl.multiple_of(res * PIECE, PIECE)

    for k, dy in enumerate(others4):
        ty = lax.rem(y + dy, NY)
        send(panel.at[0, ty], pyr.at[y], p_send.at[0], p_recv.at[0], (ty, z, x, c))
    pyr[y] = panel[0, y]
    spread(1, 16)
    drain(pyr.at[0:3], p_recv.at[0])
    psel[...] = pyr[y0]
    for k, dz in enumerate(window):
        tz = lax.rem(z + dz, NZ)
        row = pl.multiple_of(lax.rem(tz, 4) * PIECE, PIECE)
        send(
            psel.at[pl.ds(row, PIECE)], wz.at[k + 1], p_send.at[1], p_recv.at[1], (y, tz, x, c)
        )
    wz[0] = psel[pl.ds(res_row, PIECE)]
    spread(16, 32)
    drain(wz.at[0:3], p_recv.at[1])
    delta = lax.bitwise_and(z - z0, 15)
    came = jnp.where(delta == 1, 1, jnp.where(delta == 15, 2, jnp.where(delta == far2, 3, 0)))
    mz[0] = wz[came]
    for k, dz in enumerate(mates):
        send(
            mz.at[0],
            mz.at[k + 1],
            p_send.at[2],
            p_recv.at[2],
            (y, lax.rem(z + dz, NZ), x, c),
        )
    spread(32, 48)
    drain(mz.at[1:4], p_recv.at[2])
    came = jnp.int32(0)
    for k, dz in enumerate(mates):
        delta = lax.bitwise_and(z - dz - z0, 15)
        valid = (delta == 0) | (delta == 1) | (delta == 15) | (delta == far2)
        came = jnp.where(valid, k + 1, came)
    part = piv.at[u, y]
    part[pl.ds(res_row, PIECE)] = mz[came]
    for k, dz in enumerate(window):
        send(
            part.at[pl.ds(res_row, PIECE)],
            part.at[pl.ds(res_row, PIECE)],
            p_send.at[3],
            p_recv.at[3],
            (y, lax.rem(z + dz, NZ), x, c),
        )
    spread(48, 64)
    drain(mz.at[1:4], p_recv.at[3])
    for k, dy in enumerate(others4):
        send(part, part, p_send.at[4], p_recv.at[4], (lax.rem(y + dy, NY), z, x, c))
    drain(pyr.at[0:3], p_recv.at[4])
    strip = piv.at[u]
    for k, dx in enumerate(others4):
        send(strip, strip, p_send.at[5], q_recv.at[k], (y, z, lax.rem(x + dx, NX), c))
    send(strip, strip, q_send, p_recv.at[5], (y, z, x, 1 - c))

    a2r[me] = panel[y, res, pl.ds(my_row, PIECE)]
    drain(a2r.at[0 : TRI - 1], a_recv)
    gathered = yb.at[y]
    for g in range(GROUPS):
        gathered[g, pl.ds(my_row, PIECE)] = a2r[owner_ref[g * GROUPS]]
    for k, dz in enumerate(mates):
        piece = gathered.at[:, pl.ds(my_row, PIECE)]
        send(piece, piece, m_send, m_recv, (y, lax.rem(z + dz, NZ), x, c))

    for k, dx in enumerate(others4):
        drain(strip, q_recv.at[k])
        source = lax.rem(x - dx + NX, NX) * NC + c
        send(piv.at[source], piv.at[source], q_send, p_recv.at[5], (y, z, x, 1 - c))

    drain(gathered.at[:, 0 : 3 * PIECE], m_recv)
    for k, dy in enumerate(others4):
        send(gathered, gathered, y_send, y_recv, (lax.rem(y + dy, NY), z, x, c))
    drain(piv.at[0:4], p_recv.at[5])
    whole_pivot(piv, p)
    newton_start(p, xb, yv)
    newton_steps(p, xb, yv, 0, 1)
    drain(yb.at[0:3], y_recv)

    def pick(cell, out):
        row_group, col_group, first = groups_of(cell)
        for i in range(PER):
            out[i] = yb[i, row_group]
        for j in range(2):
            out[PER + j] = yb[first + j, col_group]

    for k, dz in enumerate(window):
        pick(cells[k + 1], msg.at[k])
        send(
            msg.at[k], fin.at[res], w_send, w_recv.at[k], (y, lax.rem(z + dz, NZ), x, c)
        )
    pick(cells[0], fin.at[res])
    newton_steps(p, xb, yv, 1, 4)

    for part_no in range(4):
        if part_no > 0:
            drain(msg.at[0], w_recv.at[part_no - 1])
        b = lax.rem(z - (0, 1, 15, far2)[part_no] + NZ, 4)
        right[u, b] = fin[b, 2:6]
        for k, dx in enumerate(others4):
            send(
                fin.at[b, 2:6],
                right.at[u, b],
                x_send,
                x_recv.at[part_no, k],
                (y, z, lax.rem(x + dx, NX), c),
            )
        send(fin.at[b, 2:6], right.at[u, b], c_send, c_recv, (y, z, x, 1 - c))
    newton_steps(p, xb, yv, 4, 6)
    yv[...] = jnp.where(identity(), 1.0, 0.0) - yv[...]
    size_ref[...] = jnp.broadcast_to(jnp.sum(yv[...] * yv[...]), size_ref.shape)
    xf[...] = xb[...].astype(F32)
    refine(xb, xl, xf, yv)
    for part_no in range(4):
        b = lax.rem(z - (0, 1, 15, far2)[part_no] + NZ, 4)
        for k, dx in enumerate(others4):
            drain(right.at[0, 0], x_recv.at[part_no, k])
            source = lax.rem(x - dx + NX, NX) * NC + c
            send(right.at[source, b], right.at[source, b], c_send, c_recv, (y, z, x, 1 - c))
    drain(right.at[0:4], c_recv)

    drain(pyr.at[0:3], p_send.at[0])
    drain(wz.at[0:3], p_send.at[1])
    drain(mz.at[1:4], p_send.at[2])
    drain(mz.at[1:4], p_send.at[3])
    drain(pyr.at[0:3], p_send.at[4])
    drain(piv.at[0:3], p_send.at[5])
    drain(piv.at[0:4], q_send)
    drain(a2r.at[0 : TRI - 1], a_send)
    drain(gathered.at[:, 0 : 3 * PIECE], m_send)
    drain(yb.at[0:3], y_send)
    drain(msg, w_send)
    drain(right.at[0:3], x_send)
    drain(right.at[0:4], c_send)


def dot(a, b, precision=None):
    return lax.dot_general(
        a, b, (((1,), (0,)), ((), ())), precision=precision, preferred_element_type=F32
    )


def dot_nt(a, b):
    return lax.dot_general(a, b, (((1,), (1,)), ((), ())), preferred_element_type=F32)


def schedule(low, steps):
    out, scale = [], 1.0
    for _ in range(steps):
        s = (1 + low) / (1 - low)
        t = 2 * s * s - 1
        out.append((8 * (1 + low) / (1 - low) ** 2 / t / scale, 8 / (1 - low) ** 2 / t / scale**2))
        scale, low = 1 + 1 / t, (1 - 1 / t) / (1 + 1 / t)
    return out


def identity():
    shape = (N, N)
    return lax.broadcasted_iota(jnp.int32, shape, 0) == lax.broadcasted_iota(jnp.int32, shape, 1)


COEFS = schedule(NEWTON_LOW, NEWTON_STEPS)


def whole_pivot(piv, p):
    for v in range(SUB):
        for b in range(CB):
            p[v * ROWS : (v + 1) * ROWS, b * LANES : (b + 1) * LANES] = piv[v, b]


def newton_start(p, xb, yv):
    yv[...] = dot_nt(p[...], p[...])
    bound = jnp.max(jnp.sum(jnp.abs(yv[...]), axis=0, keepdims=True))
    inv = 1.0 / bound
    xb[...] = (p[...].astype(F32) * -inv).astype(BF)
    yv[...] = yv[...] * inv


def newton_steps(p, xb, yv, lo, hi):
    def step(k, carry):
        c1, c2 = jnp.float32(COEFS[lo][0]), jnp.float32(COEFS[lo][1])
        for i in range(lo + 1, hi):
            c1 = jnp.where(k == i, COEFS[i][0], c1)
            c2 = jnp.where(k == i, COEFS[i][1], c2)
        m = (jnp.where(identity(), c1, 0.0) - c2 * yv[...]).astype(BF)
        xb[...] = dot(xb[...], m).astype(BF)
        yv[...] = dot(p[...], xb[...])
        return carry

    lax.fori_loop(lo, hi, step, 0)


def refine(xb, xl, xf, yv):
    small = yv[...].astype(BF)
    yv[...] = yv[...] + dot(small, small)
    better = xf[...] + dot(xf[...].astype(BF), yv[...].astype(BF))
    high = better.astype(BF)
    xb[...] = high
    xl[...] = (better - high.astype(F32)).astype(BF)


def update_kernel(
    owner_ref,
    tiles_ref,
    fin,
    right,
    xb_in,
    xl_in,
    size_ref,
    piv_any,
    out_ref,
    cur,
    xb,
    xl,
    p,
    piv,
    xf,
    yv,
    rt,
    left,
    in_sem,
    out_sem,
    piv_sem,
):
    for slot in range(10):
        pltpu.make_async_copy(tiles_ref.at[0, slot], cur.at[slot], in_sem.at[slot]).start()
    me = lax.axis_index("y") * NZ + lax.axis_index("z")
    (cell,) = cells_at(owner_ref, (me,))
    row_group, col_group, first = groups_of(cell)
    diagonal = row_group == col_group
    good = jnp.max(size_ref[...]) < 0.01

    @pl.when(good)
    def _():
        xb[...] = xb_in[...]
        xl[...] = xl_in[...]

    @pl.when(jnp.logical_not(good))
    def _():
        copy = pltpu.make_async_copy(piv_any, piv, piv_sem)
        copy.start()
        copy.wait()
        whole_pivot(piv, p)
        highest = lax.Precision.HIGHEST
        whole = p[...].astype(F32)
        rows = jnp.max(jnp.sum(jnp.abs(whole), axis=0, keepdims=True))
        xf[...] = whole * (-1.0 / rows) / rows

        def residual():
            yv[...] = jnp.where(identity(), 1.0, 0.0) - dot(p[...].astype(F32), xf[...], highest)
            return jnp.sum(yv[...] * yv[...])

        def more(carry):
            k, _ = carry
            xf[...] = xf[...] + dot(xf[...], yv[...], highest)
            return k + 1, residual()

        lax.while_loop(lambda s: (s[0] < 150) & (s[1] > 0.001), more, (0, residual()))
        refine(xb, xl, xf, yv)

    for i in range(PER):
        strip = jnp.concatenate([fin[b, i] for b in range(CB)], axis=1)
        left[i * ROWS : (i + 1) * ROWS] = (
            dot(strip, xb[...]) + dot(strip, xl[...])
        ).astype(BF)

    def stage(j, strip):
        for v in range(SUB):
            for b in range(CB):
                rt[j, v * ROWS : (v + 1) * ROWS, b * LANES : (b + 1) * LANES] = right[v, b, strip]

    for slot in range(10):
        pltpu.make_async_copy(tiles_ref.at[0, slot], cur.at[slot], in_sem.at[slot]).wait()
    stage(0, 2)
    stage(1, 3)

    @pl.when(diagonal)
    def _():
        stage(2, 0)
        stage(3, 1)
        for j in range(PER):
            live = (row_group > 0) | (j > 0)
            product = dot_nt(left[j * ROWS :], rt[j])
            for i in range(j, PER):
                slot = i * (i + 1) // 2 + j
                term = product[(i - j) * ROWS : (i - j + 1) * ROWS]
                cur[slot] = cur[slot] + jnp.where(live, term, 0.0)

    @pl.when(jnp.logical_not(diagonal))
    def _():
        for j in range(2):
            live = col_group * PER + first + j > 0
            product = dot_nt(left[...], rt[j])
            for i in range(PER):
                slot = 2 * i + j
                term = product[i * ROWS : (i + 1) * ROWS]
                cur[slot] = cur[slot] + jnp.where(live, term, 0.0)

    for slot in range(10):
        pltpu.make_async_copy(cur.at[slot], out_ref.at[0, slot], out_sem.at[slot]).start()
    for slot in range(10):
        pltpu.make_async_copy(cur.at[slot], out_ref.at[0, slot], out_sem.at[slot]).wait()


def shards(stored_tiles, cell_owner):
    dma = pltpu.SemaphoreType.DMA
    vmem = pl.BlockSpec(memory_space=pltpu.VMEM)
    smem = pl.BlockSpec(memory_space=pltpu.SMEM)
    hbm = pl.BlockSpec(memory_space=pl.ANY)
    strip = (ROWS, LANES)
    stored_tiles = pltpu.with_memory_space_constraint(stored_tiles, pltpu.HBM)
    square = pltpu.VMEM((N, N), BF)
    square32 = pltpu.VMEM((N, N), F32)
    fin, right, piv, xb, xl, size = pl.pallas_call(
        route_kernel,
        out_shape=(
            jax.ShapeDtypeStruct((CB, 6, *strip), BF),
            jax.ShapeDtypeStruct((SUB, CB, 4, *strip), BF),
            jax.ShapeDtypeStruct((SUB, CB, *strip), BF),
            jax.ShapeDtypeStruct((N, N), BF),
            jax.ShapeDtypeStruct((N, N), BF),
            jax.ShapeDtypeStruct((8, LANES), F32),
        ),
        in_specs=[smem, hbm],
        out_specs=(vmem, vmem, vmem, vmem, vmem, vmem),
        scratch_shapes=[
            square,
            square32,
            square32,
            pltpu.VMEM((len(LOAD_SLOTS), ROWS, N), F32),
            pltpu.VMEM((PER, CB, *strip), BF),
            pltpu.VMEM((TRI, PIECE, LANES), BF),
            pltpu.VMEM((PER, GROUPS, *strip), BF),
            pltpu.VMEM((3, 6, *strip), BF),
            pltpu.VMEM((NY, *strip), BF),
            pltpu.VMEM(strip, BF),
            pltpu.VMEM((4, PIECE, LANES), BF),
            pltpu.VMEM((4, PIECE, LANES), BF),
            dma,
            dma((6,)),
            dma((6,)),
            dma,
            dma,
            dma,
            dma,
            dma,
            dma,
            dma,
            dma((3,)),
            dma,
            dma((4, 3)),
            dma,
            dma,
            dma,
            dma((3,)),
        ],
        compiler_params=pltpu.CompilerParams(
            collective_id=0, has_side_effects=True, vmem_limit_bytes=40 * 2**20
        ),
    )(cell_owner, stored_tiles)
    return pl.pallas_call(
        update_kernel,
        out_shape=jax.ShapeDtypeStruct(stored_tiles.shape, F32),
        in_specs=[smem, hbm, vmem, vmem, vmem, vmem, vmem, hbm],
        out_specs=hbm,
        scratch_shapes=[
            pltpu.VMEM((10, ROWS, N), F32),
            square,
            square,
            square,
            pltpu.VMEM((SUB, CB, *strip), BF),
            square32,
            square32,
            pltpu.VMEM((PER, N, N), BF),
            pltpu.VMEM((PER * ROWS, N), BF),
            dma((10,)),
            dma((10,)),
            dma,
        ],
        compiler_params=pltpu.CompilerParams(vmem_limit_bytes=40 * 2**20),
    )(cell_owner, stored_tiles, fin, right, xb, xl, size, piv)


def solution(mesh):
    torus = Mesh(mesh.devices.reshape(NY, NZ, NX, NC), AXES)
    spec = P(("y", "z"), None, ("x", "c"), None)
    return jax.shard_map(
        shards, mesh=torus, in_specs=(spec, P()), out_specs=spec, check_vma=False
    )
```

```python
import jax
import jax.numpy as jnp
from jax import lax
from jax.experimental import pallas as pl
from jax.experimental.pallas import tpu as pltpu
from jax.sharding import Mesh
from jax.sharding import PartitionSpec as P

MESH = pl.DeviceIdType.MESH
AXES = ("y", "z", "x", "c")
NY, NZ, NX, NC = 4, 16, 4, 2
TRI = NY * NZ
SUB = NX * NC
GROUPS = 8
PER = 4
SLOTS = 10
N = 512
ROWS = N // SUB
LANES = 128
CB = N // LANES
PIECE = 16
LOAD_SLOTS = (0, 1, 2, 3, 4, 6)
FIRST_SLOTS = (0, 1, 3, 6)
PAIRS = tuple((i, j) for i in range(PER) for j in range(i + 1))
NEWTON_STEPS = 6
NEWTON_LOW = 0.004
SMALL = 0.01
BF = jnp.bfloat16
F32 = jnp.float32


def drain(ref, sem):
    pltpu.make_async_copy(ref, ref, sem).wait()


def send(src, dst, send_sem, recv_sem, device):
    pltpu.make_async_remote_copy(
        src_ref=src,
        dst_ref=dst,
        send_sem=send_sem,
        recv_sem=recv_sem,
        device_id=device,
        device_id_type=MESH,
    ).start()


def cells_at(owner_ref, places):
    def body(c, found):
        owner = owner_ref[c]
        return tuple(jnp.where(owner == t, c, f) for t, f in zip(places, found))

    zero = jnp.int32(0)
    return lax.fori_loop(0, TRI, body, tuple(zero for _ in places))


def groups_of(cell):
    down = lax.shift_right_logical(cell, jnp.int32(3))
    across = lax.bitwise_and(cell, jnp.int32(7))
    first = jnp.where(down < across, 2, 0)
    return jnp.maximum(down, across), jnp.minimum(down, across), first


def dot(a, b, precision=None):
    return lax.dot_general(
        a, b, (((1,), (0,)), ((), ())), precision=precision, preferred_element_type=F32
    )


def dot_nt(a, b):
    return lax.dot_general(a, b, (((1,), (1,)), ((), ())), preferred_element_type=F32)


def schedule(low, steps):
    out, scale = [], 1.0
    for _ in range(steps):
        s = (1 + low) / (1 - low)
        t = 2 * s * s - 1
        out.append((8 * (1 + low) / (1 - low) ** 2 / t / scale, 8 / (1 - low) ** 2 / t / scale**2))
        scale, low = 1 + 1 / t, (1 - 1 / t) / (1 + 1 / t)
    return out


COEFS = schedule(NEWTON_LOW, NEWTON_STEPS)


def identity():
    shape = (N, N)
    return lax.broadcasted_iota(jnp.int32, shape, 0) == lax.broadcasted_iota(jnp.int32, shape, 1)


def whole_pivot(piv, p):
    for v in range(SUB):
        for b in range(CB):
            p[v * ROWS : (v + 1) * ROWS, b * LANES : (b + 1) * LANES] = piv[v, b]


def newton_start(p, xb, yv):
    yv[...] = dot_nt(p[...], p[...])
    bound = jnp.max(jnp.sum(jnp.abs(yv[...]), axis=0, keepdims=True))
    inv = 1.0 / bound
    xb[...] = (p[...].astype(F32) * -inv).astype(BF)
    yv[...] = yv[...] * inv


def newton_steps(p, xb, yv, lo, hi):
    def step(k, carry):
        c1, c2 = jnp.float32(COEFS[lo][0]), jnp.float32(COEFS[lo][1])
        for i in range(lo + 1, hi):
            c1 = jnp.where(k == i, COEFS[i][0], c1)
            c2 = jnp.where(k == i, COEFS[i][1], c2)
        m = (jnp.where(identity(), c1, 0.0) - c2 * yv[...]).astype(BF)
        xb[...] = dot(xb[...], m).astype(BF)
        yv[...] = dot(p[...], xb[...])
        return carry

    lax.fori_loop(lo, hi, step, 0)


def refine(xb, xl, xf, yv):
    small = yv[...].astype(BF)
    yv[...] = yv[...] + dot(small, small)
    better = xf[...] + dot(xf[...].astype(BF), yv[...].astype(BF))
    high = better.astype(BF)
    xb[...] = high
    xl[...] = (better - high.astype(F32)).astype(BF)


def scale_rows(fin, xb, xl, left):
    for i in range(PER):
        strip = jnp.concatenate([fin[b, 0, i] for b in range(CB)], axis=1)
        left[i * ROWS : (i + 1) * ROWS] = (dot(strip, xb[...]) + dot(strip, xl[...])).astype(BF)


def products(left, right, rt, us):
    for j in range(PER):
        for v in range(SUB):
            for b in range(CB):
                rt[v * ROWS : (v + 1) * ROWS, b * LANES : (b + 1) * LANES] = right[v, b, j]
        product = dot_nt(left[...], rt[...])
        for i in range(PER):
            us[j, i] = product[i * ROWS : (i + 1) * ROWS]


def add_products(cell, us, cur, slot):
    row_group, col_group, first = groups_of(cell)
    diagonal = row_group == col_group
    i, j = PAIRS[slot]
    half = min(slot, 7)
    i = jnp.where(diagonal, i, half // 2)
    j = jnp.where(diagonal, j, first + half % 2)
    live = (col_group > 0) | (j > 0)
    if slot > 7:
        live = live & diagonal
    cur[slot] = cur[slot] + jnp.where(live, us[j, i], 0.0)


def route_kernel(
    owner_ref,
    tiles_ref,
    upd,
    size_ref,
    fin_out,
    right_out,
    piv_out,
    cur,
    panel,
    a2r,
    gath0,
    gath1,
    gath2,
    gath3,
    msg,
    fin,
    right,
    piv,
    wz,
    mz,
    p,
    xb,
    xl,
    xf,
    yv,
    left,
    rt,
    us,
    load_sem,
    p_send,
    p_recv,
    a_send,
    a_recv,
    m_send,
    m_recv,
    w_send,
    w_recv,
    x_send,
    x_recv,
    c_send,
    c_recv,
    q_send,
    q_recv,
    o_sem,
    k_sem,
):
    y, z = lax.axis_index("y"), lax.axis_index("z")
    x, c = lax.axis_index("x"), lax.axis_index("c")
    me = y * NZ + z
    u = x * NC + c
    res = lax.rem(z, 4)
    quo = z // 4
    far2 = 2 + 12 * c
    window = (0, 1, 15, far2)
    mates = (0, 4, 12, 8)
    others4 = (2, 1, 3)
    gath = (gath0, gath1, gath2, gath3)
    near = [(dy, k) for k in range(4) for dy in (2, 1, 3, 0) if (dy, k) != (0, 0)]
    sibling = (y, z, x, 1 - c)

    def at_tri(dy, dz):
        return (lax.rem(y + dy, NY), lax.rem(z + dz, NZ), x, c)

    def at_x(dx):
        return (y, z, lax.rem(x + dx, NX), c)

    def from_x(dx):
        return lax.rem(x - dx + NX, NX) * NC + c

    for slot in LOAD_SLOTS:
        pltpu.make_async_copy(tiles_ref.at[0, slot], cur.at[slot], load_sem.at[slot]).start()

    barrier = pltpu.get_barrier_semaphore()

    def greet(k, carry):
        pl.semaphore_signal(
            barrier, inc=1, device_id=at_tri(k // NZ, lax.rem(k, NZ)), device_id_type=MESH
        )
        return carry

    lax.fori_loop(1, TRI, greet, 0)
    for d in others4:
        pl.semaphore_signal(barrier, inc=1, device_id=at_x(d), device_id_type=MESH)
    pl.semaphore_signal(barrier, inc=1, device_id=sibling, device_id_type=MESH)
    for slot in range(SLOTS):
        if slot not in LOAD_SLOTS:
            pltpu.make_async_copy(tiles_ref.at[0, slot], cur.at[slot], load_sem.at[slot]).start()

    (cell,) = cells_at(owner_ref, (me,))
    pivot_at = owner_ref[0]
    y0 = lax.shift_right_logical(pivot_at, jnp.int32(4))
    z0 = lax.bitwise_and(pivot_at, jnp.int32(15))
    for slot in LOAD_SLOTS:
        pltpu.make_async_copy(tiles_ref.at[0, slot], cur.at[slot], load_sem.at[slot]).wait()
    is_first = cell < GROUPS
    for i in range(PER):
        tile = jnp.where(is_first, cur[FIRST_SLOTS[i]], cur[2 * i]).astype(BF)
        for b in range(CB):
            panel[i, b] = tile[:, b * LANES : (b + 1) * LANES]
    cells = {(0, 0): cell}
    found = cells_at(owner_ref, tuple(
        lax.rem(y + dy, NY) * NZ + lax.rem(z + window[k], NZ) for dy, k in near
    ))
    cells.update(zip(near, found))
    pl.semaphore_wait(barrier, TRI - 1 + 4)

    my_row = pl.multiple_of(quo * PIECE, PIECE)
    res_row = pl.multiple_of(res * PIECE, PIECE)
    for dy, k in near:
        ty, tz, _, _ = at_tri(dy, window[k])
        row = pl.multiple_of(lax.rem(tz, 4) * PIECE, PIECE)
        send(
            panel.at[0, ty, pl.ds(row, PIECE)],
            wz.at[dy * 4 + k],
            p_send.at[0],
            p_recv.at[0],
            (ty, tz, x, c),
        )
    wz[0] = panel[0, y, pl.ds(res_row, PIECE)]

    def spread(dy, dz):
        ty, tz, _, _ = at_tri(dy, dz)
        row = pl.multiple_of((tz // 4) * PIECE, PIECE)
        send(
            panel.at[ty, lax.rem(tz, 4), pl.ds(row, PIECE)],
            a2r.at[me],
            a_send,
            a_recv,
            (ty, tz, x, c),
        )

    def spread_all(k, carry):
        spread(k // NZ, lax.rem(k, NZ))
        return carry

    lax.fori_loop(1, TRI, spread_all, 0)
    a2r[me] = panel[y, res, pl.ds(my_row, PIECE)]

    def near_to(delta):
        return (delta == 0) | (delta == 1) | (delta == 15) | (delta == far2)

    drain(wz.at[1:16], p_recv.at[0])
    delta = lax.bitwise_and(z - z0, 15)
    came = jnp.where(delta == 1, 1, jnp.where(delta == 15, 2, jnp.where(delta == far2, 3, 0)))
    mz[0] = wz[lax.bitwise_and(y - y0, 3) * 4 + came]
    for k in range(1, 4):
        send(mz.at[0], mz.at[k], p_send.at[1], p_recv.at[1], at_tri(0, mates[k]))
    drain(mz.at[1:4], p_recv.at[1])
    came = jnp.int32(0)
    for k in range(1, 4):
        delta = lax.bitwise_and(z - mates[k] - z0, 15)
        came = jnp.where(near_to(delta), k, came)
    part = piv.at[u, y, pl.ds(res_row, PIECE)]
    part[...] = mz[came]
    for dy, k in near:
        send(part, part, p_send.at[2], p_recv.at[2], at_tri(dy, window[k]))

    drain(a2r.at[0 : TRI - 1], a_recv)
    for g in range(GROUPS):
        gath0[g] = a2r[owner_ref[g * GROUPS]]
    for k in (3, 1, 2):
        send(gath0, gath[k], m_send, m_recv.at[k], at_tri(0, mates[k]))

    def row_of(place):
        return pl.multiple_of((lax.rem(place + 2 * NZ, NZ) // 4) * PIECE, PIECE)

    def hand_out(q):
        row = row_of(z - mates[q])
        for n, (dy, k) in enumerate(near):
            row_group, col_group, _ = groups_of(cells[dy, k])
            msg[q, n, 0] = gath[q][row_group]
            msg[q, n, 1] = gath[q][col_group]
            send(
                msg.at[q, n],
                fin.at[res, :, y, pl.ds(row, PIECE)],
                w_send,
                w_recv.at[q, k],
                at_tri(dy, window[k]),
            )
        row_group, col_group, _ = groups_of(cell)
        fin[res, 0, y, pl.ds(row, PIECE)] = gath[q][row_group]
        fin[res, 1, y, pl.ds(row, PIECE)] = gath[q][col_group]

    def part_of(q, k):
        source = z - window[k]
        b = lax.rem(source + NZ, 4)
        return b, row_of(source - mates[q])

    def over_x(q):
        for k in range(4):
            drain(msg.at[0, 0 : 3 if k == 0 else 4], w_recv.at[q, k])
            b, row = part_of(q, k)
            rows = pl.ds(row, PIECE)
            for n, dx in enumerate(others4):
                send(
                    fin.at[b, 1, :, rows],
                    right.at[u, b, :, rows],
                    x_send,
                    x_recv.at[q, n],
                    at_x(dx),
                )
            send(fin.at[b, 1, :, rows], right.at[u, b, :, rows], c_send, c_recv, sibling)

    def over_core(q):
        for n in (1, 2, 0):
            drain(right.at[0, :, :, 0:PIECE], x_recv.at[q, n])
            source = from_x(others4[n])
            for k in range(4):
                b, row = part_of(q, k)
                there = right.at[source, b, :, pl.ds(row, PIECE)]
                send(there, there, c_send, c_recv, sibling)

    hand_out(0)
    drain(wz.at[1:16], p_recv.at[2])
    strip = piv.at[u]
    for n, dx in enumerate(others4):
        send(strip, strip, p_send.at[3], q_recv.at[n], at_x(dx))
    send(strip, strip, q_send, p_recv.at[3], sibling)
    for q in (1, 2):
        drain(gath[q], m_recv.at[q])
        hand_out(q)
    over_x(0)
    for n in (1, 2, 0):
        drain(strip, q_recv.at[n])
        there = piv.at[from_x(others4[n])]
        send(there, there, q_send, p_recv.at[3], sibling)
    drain(gath[3], m_recv.at[3])
    hand_out(3)
    drain(piv.at[0:4], p_recv.at[3])
    whole_pivot(piv, p)
    keep_piv = pltpu.make_async_copy(piv, piv_out, k_sem.at[0])
    keep_piv.start()
    newton_start(p, xb, yv)
    over_x(1)
    over_x(2)
    newton_steps(p, xb, yv, 0, 2)
    over_core(0)
    over_x(3)
    for b in range(CB):
        right[u, b] = fin[b, 1]
    keep_fin = pltpu.make_async_copy(fin, fin_out, k_sem.at[1])
    keep_fin.start()
    newton_steps(p, xb, yv, 2, 4)
    over_core(1)
    over_core(2)
    newton_steps(p, xb, yv, 4, 6)
    over_core(3)

    yv[...] = jnp.where(identity(), 1.0, 0.0) - yv[...]
    size_ref[...] = jnp.broadcast_to(jnp.sum(yv[...] * yv[...]), size_ref.shape)
    xf[...] = xb[...].astype(F32)
    refine(xb, xl, xf, yv)
    scale_rows(fin, xb, xl, left)

    drain(right.at[0:4], c_recv)
    keep_right = pltpu.make_async_copy(right, right_out, k_sem.at[2])
    keep_right.start()
    products(left, right, rt, us)
    for slot in range(SLOTS):
        if slot not in LOAD_SLOTS:
            pltpu.make_async_copy(tiles_ref.at[0, slot], cur.at[slot], load_sem.at[slot]).wait()
        add_products(cell, us, cur, slot)
        pltpu.make_async_copy(cur.at[slot], upd.at[0, slot], o_sem.at[slot]).start()

    drain(wz.at[1:16], p_send.at[0])
    drain(mz.at[1:4], p_send.at[1])
    drain(wz.at[1:16], p_send.at[2])
    drain(piv.at[0:3], p_send.at[3])
    drain(piv.at[0:4], q_send)
    drain(a2r.at[0 : TRI - 1], a_send)
    drain(a2r.at[0 : 3 * GROUPS], m_send)
    drain(msg, w_send)
    drain(right.at[0:3], x_send)
    drain(right.at[0:4], c_send)
    keep_piv.wait()
    keep_fin.wait()
    keep_right.wait()
    for slot in range(SLOTS):
        pltpu.make_async_copy(cur.at[slot], upd.at[0, slot], o_sem.at[slot]).wait()


def result_kernel(
    size_ref,
    owner_any,
    tiles_ref,
    upd,
    fin_any,
    right_any,
    piv_any,
    out_ref,
    owner_ref,
    cur,
    fin,
    right,
    piv,
    p,
    xb,
    xl,
    xf,
    yv,
    left,
    rt,
    us,
    sem,
    out_sem,
):
    good = jnp.max(size_ref[...]) < SMALL

    @pl.when(good)
    def _():
        for slot in range(SLOTS):
            pltpu.make_async_copy(upd.at[0, slot], out_ref.at[0, slot], out_sem.at[slot]).start()
        for slot in range(SLOTS):
            pltpu.make_async_copy(upd.at[0, slot], out_ref.at[0, slot], out_sem.at[slot]).wait()

    @pl.when(jnp.logical_not(good))
    def _():
        pairs = (
            (owner_any, owner_ref),
            (tiles_ref.at[0], cur),
            (fin_any, fin),
            (right_any, right),
            (piv_any, piv),
        )
        for n, (src, dst) in enumerate(pairs):
            copy = pltpu.make_async_copy(src, dst, sem.at[n])
            copy.start()
            copy.wait()
        me = lax.axis_index("y") * NZ + lax.axis_index("z")
        (cell,) = cells_at(owner_ref, (me,))
        whole_pivot(piv, p)
        highest = lax.Precision.HIGHEST
        whole = p[...].astype(F32)
        rows = jnp.max(jnp.sum(jnp.abs(whole), axis=0, keepdims=True))
        xf[...] = whole * (-1.0 / rows) / rows

        def residual():
            yv[...] = jnp.where(identity(), 1.0, 0.0) - dot(p[...].astype(F32), xf[...], highest)
            return jnp.sum(yv[...] * yv[...])

        def more(carry):
            k, _ = carry
            xf[...] = xf[...] + dot(xf[...], yv[...], highest)
            return k + 1, residual()

        lax.while_loop(lambda s: (s[0] < 150) & (s[1] > 0.001), more, (0, residual()))
        refine(xb, xl, xf, yv)
        scale_rows(fin, xb, xl, left)
        products(left, right, rt, us)
        for slot in range(SLOTS):
            add_products(cell, us, cur, slot)
            copy = pltpu.make_async_copy(cur.at[slot], out_ref.at[0, slot], out_sem.at[slot])
            copy.start()
            copy.wait()


def shards(stored_tiles, cell_owner):
    dma = pltpu.SemaphoreType.DMA
    vmem = pl.BlockSpec(memory_space=pltpu.VMEM)
    anywhere = pl.BlockSpec(memory_space=pl.ANY)
    hbm = pl.BlockSpec(memory_space=pltpu.HBM)
    strip = (ROWS, LANES)
    fin_shape = (CB, 2, PER, *strip)
    right_shape = (SUB, CB, PER, *strip)
    piv_shape = (SUB, CB, *strip)
    work = [
        pltpu.VMEM((N, N), BF),
        pltpu.VMEM((N, N), BF),
        pltpu.VMEM((N, N), BF),
        pltpu.VMEM((N, N), F32),
        pltpu.VMEM((N, N), F32),
        pltpu.VMEM((PER * ROWS, N), BF),
        pltpu.VMEM((N, N), BF),
        pltpu.VMEM((PER, PER, ROWS, N), F32),
    ]
    owner = pltpu.SMEM((TRI,), jnp.int32)
    stored_tiles = pltpu.with_memory_space_constraint(stored_tiles, pltpu.HBM)
    tiles = pltpu.VMEM((SLOTS, ROWS, N), F32)
    upd, size, fin, right, piv = pl.pallas_call(
        route_kernel,
        out_shape=(
            jax.ShapeDtypeStruct(stored_tiles.shape, F32),
            jax.ShapeDtypeStruct((8, LANES), F32),
            jax.ShapeDtypeStruct(fin_shape, BF),
            jax.ShapeDtypeStruct(right_shape, BF),
            jax.ShapeDtypeStruct(piv_shape, BF),
        ),
        in_specs=[pl.BlockSpec(memory_space=pltpu.SMEM), hbm],
        out_specs=(anywhere, vmem, hbm, hbm, hbm),
        scratch_shapes=[
            tiles,
            pltpu.VMEM((PER, CB, *strip), BF),
            pltpu.VMEM((TRI, PIECE, LANES), BF),
            pltpu.VMEM((GROUPS, PIECE, LANES), BF),
            pltpu.VMEM((GROUPS, PIECE, LANES), BF),
            pltpu.VMEM((GROUPS, PIECE, LANES), BF),
            pltpu.VMEM((GROUPS, PIECE, LANES), BF),
            pltpu.VMEM((4, 15, 2, PIECE, LANES), BF),
            pltpu.VMEM(fin_shape, BF),
            pltpu.VMEM(right_shape, BF),
            pltpu.VMEM(piv_shape, BF),
            pltpu.VMEM((16, PIECE, LANES), BF),
            pltpu.VMEM((4, PIECE, LANES), BF),
            *work,
            dma((SLOTS,)),
            dma((4,)),
            dma((4,)),
            dma,
            dma,
            dma,
            dma((4,)),
            dma,
            dma((4, 4)),
            dma,
            dma((4, 3)),
            dma,
            dma,
            dma,
            dma((3,)),
            dma((SLOTS,)),
            dma((3,)),
        ],
        compiler_params=pltpu.CompilerParams(
            collective_id=0, has_side_effects=True, vmem_limit_bytes=48 * 2**20
        ),
    )(cell_owner, stored_tiles)
    return pl.pallas_call(
        result_kernel,
        out_shape=jax.ShapeDtypeStruct(stored_tiles.shape, F32),
        in_specs=[vmem, anywhere, hbm, anywhere, hbm, hbm, hbm],
        out_specs=hbm,
        scratch_shapes=[
            owner,
            tiles,
            pltpu.VMEM(fin_shape, BF),
            pltpu.VMEM(right_shape, BF),
            pltpu.VMEM(piv_shape, BF),
            *work,
            dma((5,)),
            dma((SLOTS,)),
        ],
        compiler_params=pltpu.CompilerParams(vmem_limit_bytes=40 * 2**20),
    )(size, cell_owner, stored_tiles, upd, fin, right, piv)


def solution(mesh):
    torus = Mesh(mesh.devices.reshape(NY, NZ, NX, NC), AXES)
    spec = P(("y", "z"), None, ("x", "c"), None)
    return jax.shard_map(
        shards, mesh=torus, in_specs=(spec, P()), out_specs=spec, check_vma=False
    )
```

```python
import jax
import jax.numpy as jnp
from jax import lax
from jax.experimental import pallas as pl
from jax.experimental.pallas import tpu as pltpu
from jax.sharding import Mesh
from jax.sharding import PartitionSpec as P

MESH = pl.DeviceIdType.MESH
AXES = ("y", "z", "x", "c")
NY, NZ, NX, NC = 4, 16, 4, 2
TRI = NY * NZ
SUB = NX * NC
GROUPS = 8
PER = 4
SLOTS = 10
N = 512
ROWS = N // SUB
LANES = 128
CB = N // LANES
PIECE = 16
LOAD_SLOTS = (0, 1, 2, 3, 4, 6)
FIRST_SLOTS = (0, 1, 3, 6)
PAIRS = tuple((i, j) for i in range(PER) for j in range(i + 1))
NEWTON_STEPS = 5
NEWTON_LOW = 0.02
SMALL = 0.01
BF = jnp.bfloat16
F32 = jnp.float32


def drain(ref, sem):
    pltpu.make_async_copy(ref, ref, sem).wait()


def send(src, dst, send_sem, recv_sem, device):
    pltpu.make_async_remote_copy(
        src_ref=src,
        dst_ref=dst,
        send_sem=send_sem,
        recv_sem=recv_sem,
        device_id=device,
        device_id_type=MESH,
    ).start()


def cells_at(owner_ref, places):
    def body(c, found):
        owner = owner_ref[c]
        return tuple(jnp.where(owner == t, c, f) for t, f in zip(places, found))

    zero = jnp.int32(0)
    return lax.fori_loop(0, TRI, body, tuple(zero for _ in places))


def groups_of(cell):
    down = lax.shift_right_logical(cell, jnp.int32(3))
    across = lax.bitwise_and(cell, jnp.int32(7))
    first = jnp.where(down < across, 2, 0)
    return jnp.maximum(down, across), jnp.minimum(down, across), first


def dot(a, b, precision=None):
    return lax.dot_general(
        a, b, (((1,), (0,)), ((), ())), precision=precision, preferred_element_type=F32
    )


def dot_nt(a, b):
    return lax.dot_general(a, b, (((1,), (1,)), ((), ())), preferred_element_type=F32)


def schedule(low, steps):
    out, scale = [], 1.0
    for _ in range(steps):
        s = (1 + low) / (1 - low)
        t = 2 * s * s - 1
        out.append((8 * (1 + low) / (1 - low) ** 2 / t / scale, 8 / (1 - low) ** 2 / t / scale**2))
        scale, low = 1 + 1 / t, (1 - 1 / t) / (1 + 1 / t)
    return out


COEFS = schedule(NEWTON_LOW, NEWTON_STEPS)


def identity():
    shape = (N, N)
    return lax.broadcasted_iota(jnp.int32, shape, 0) == lax.broadcasted_iota(jnp.int32, shape, 1)


def whole_pivot(piv, p):
    for v in range(SUB):
        for b in range(CB):
            p[v * ROWS : (v + 1) * ROWS, b * LANES : (b + 1) * LANES] = piv[v, b]


def newton_start(p, xb, yv):
    yv[...] = dot_nt(p[...], p[...])
    bound = jnp.max(jnp.sum(jnp.abs(yv[...]), axis=0, keepdims=True))
    inv = 1.0 / bound
    xb[...] = (p[...].astype(F32) * -inv).astype(BF)
    yv[...] = yv[...] * inv


def newton_steps(p, xb, yv, lo, hi):
    def step(k, carry):
        c1, c2 = jnp.float32(COEFS[lo][0]), jnp.float32(COEFS[lo][1])
        for i in range(lo + 1, hi):
            c1 = jnp.where(k == i, COEFS[i][0], c1)
            c2 = jnp.where(k == i, COEFS[i][1], c2)
        m = (jnp.where(identity(), c1, 0.0) - c2 * yv[...]).astype(BF)
        xb[...] = dot(xb[...], m).astype(BF)
        yv[...] = dot(p[...], xb[...])
        return carry

    lax.fori_loop(lo, hi, step, 0)


def refine(xb, xl, xf, yv):
    small = yv[...].astype(BF)
    yv[...] = yv[...] + dot(small, small)
    better = xf[...] + dot(xf[...].astype(BF), yv[...].astype(BF))
    high = better.astype(BF)
    xb[...] = high
    xl[...] = (better - high.astype(F32)).astype(BF)


def scale_rows(fin, xb, xl, left):
    for i in range(PER):
        strip = jnp.concatenate([fin[b, 0, i] for b in range(CB)], axis=1)
        left[i * ROWS : (i + 1) * ROWS] = (dot(strip, xb[...]) + dot(strip, xl[...])).astype(BF)


def products(left, right, rt, us):
    for j in range(PER):
        for v in range(SUB):
            for b in range(CB):
                rt[v * ROWS : (v + 1) * ROWS, b * LANES : (b + 1) * LANES] = right[v, b, j]
        product = dot_nt(left[...], rt[...])
        for i in range(PER):
            us[j, i] = product[i * ROWS : (i + 1) * ROWS]


def add_products(cell, us, cur, slot):
    row_group, col_group, first = groups_of(cell)
    diagonal = row_group == col_group
    i, j = PAIRS[slot]
    half = min(slot, 7)
    i = jnp.where(diagonal, i, half // 2)
    j = jnp.where(diagonal, j, first + half % 2)
    live = (col_group > 0) | (j > 0)
    if slot > 7:
        live = live & diagonal
    cur[slot] = cur[slot] + jnp.where(live, us[j, i], 0.0)


def route_kernel(
    owner_ref,
    tiles_ref,
    upd,
    size_ref,
    fin_out,
    right_out,
    piv_out,
    cur,
    panel,
    a2r,
    gath0,
    gath1,
    gath2,
    gath3,
    msg,
    fin,
    right,
    piv,
    wz,
    mz,
    p,
    xb,
    xl,
    xf,
    yv,
    left,
    rt,
    us,
    load_sem,
    p_send,
    p_recv,
    a_send,
    a_recv,
    m_send,
    m_recv,
    w_send,
    w_recv,
    x_send,
    x_recv,
    c_send,
    c_recv,
    q_send,
    q_recv,
    o_sem,
    k_sem,
):
    y, z = lax.axis_index("y"), lax.axis_index("z")
    x, c = lax.axis_index("x"), lax.axis_index("c")
    me = y * NZ + z
    u = x * NC + c
    res = lax.rem(z, 4)
    quo = z // 4
    far2 = 2 + 12 * c
    window = (0, 1, 15, far2)
    mates = (0, 4, 12, 8)
    others4 = (2, 1, 3)
    gath = (gath0, gath1, gath2, gath3)
    near = [(dy, k) for k in range(4) for dy in (2, 1, 3, 0) if (dy, k) != (0, 0)]
    sibling = (y, z, x, 1 - c)

    def at_tri(dy, dz):
        return (lax.rem(y + dy, NY), lax.rem(z + dz, NZ), x, c)

    def at_x(dx):
        return (y, z, lax.rem(x + dx, NX), c)

    def from_x(dx):
        return lax.rem(x - dx + NX, NX) * NC + c

    for slot in LOAD_SLOTS:
        pltpu.make_async_copy(tiles_ref.at[0, slot], cur.at[slot], load_sem.at[slot]).start()

    barrier = pltpu.get_barrier_semaphore()

    def greet(k, carry):
        pl.semaphore_signal(
            barrier, inc=1, device_id=at_tri(k // NZ, lax.rem(k, NZ)), device_id_type=MESH
        )
        return carry

    lax.fori_loop(1, TRI, greet, 0)
    for d in others4:
        pl.semaphore_signal(barrier, inc=1, device_id=at_x(d), device_id_type=MESH)
    pl.semaphore_signal(barrier, inc=1, device_id=sibling, device_id_type=MESH)
    for slot in range(SLOTS):
        if slot not in LOAD_SLOTS:
            pltpu.make_async_copy(tiles_ref.at[0, slot], cur.at[slot], load_sem.at[slot]).start()

    (cell,) = cells_at(owner_ref, (me,))
    pivot_at = owner_ref[0]
    y0 = lax.shift_right_logical(pivot_at, jnp.int32(4))
    z0 = lax.bitwise_and(pivot_at, jnp.int32(15))
    for slot in LOAD_SLOTS:
        pltpu.make_async_copy(tiles_ref.at[0, slot], cur.at[slot], load_sem.at[slot]).wait()
    is_first = cell < GROUPS
    for i in range(PER):
        tile = jnp.where(is_first, cur[FIRST_SLOTS[i]], cur[2 * i]).astype(BF)
        for b in range(CB):
            panel[i, b] = tile[:, b * LANES : (b + 1) * LANES]
    cells = {(0, 0): cell}
    found = cells_at(owner_ref, tuple(
        lax.rem(y + dy, NY) * NZ + lax.rem(z + window[k], NZ) for dy, k in near
    ))
    cells.update(zip(near, found))
    pl.semaphore_wait(barrier, TRI - 1 + 4)

    my_row = pl.multiple_of(quo * PIECE, PIECE)
    res_row = pl.multiple_of(res * PIECE, PIECE)
    for dy, k in near:
        ty, tz, _, _ = at_tri(dy, window[k])
        row = pl.multiple_of(lax.rem(tz, 4) * PIECE, PIECE)
        send(
            panel.at[0, ty, pl.ds(row, PIECE)],
            wz.at[dy * 4 + k],
            p_send.at[0],
            p_recv.at[0],
            (ty, tz, x, c),
        )
    wz[0] = panel[0, y, pl.ds(res_row, PIECE)]

    def spread(dy, dz):
        ty, tz, _, _ = at_tri(dy, dz)
        row = pl.multiple_of((tz // 4) * PIECE, PIECE)
        send(
            panel.at[ty, lax.rem(tz, 4), pl.ds(row, PIECE)],
            a2r.at[me],
            a_send,
            a_recv,
            (ty, tz, x, c),
        )

    def spread_all(k, carry):
        spread(k // NZ, lax.rem(k, NZ))
        return carry

    lax.fori_loop(1, TRI, spread_all, 0)
    a2r[me] = panel[y, res, pl.ds(my_row, PIECE)]

    def near_to(delta):
        return (delta == 0) | (delta == 1) | (delta == 15) | (delta == far2)

    drain(wz.at[1:16], p_recv.at[0])
    delta = lax.bitwise_and(z - z0, 15)
    came = jnp.where(delta == 1, 1, jnp.where(delta == 15, 2, jnp.where(delta == far2, 3, 0)))
    mz[0] = wz[lax.bitwise_and(y - y0, 3) * 4 + came]
    for k in range(1, 4):
        send(mz.at[0], mz.at[k], p_send.at[1], p_recv.at[1], at_tri(0, mates[k]))
    drain(mz.at[1:4], p_recv.at[1])
    came = jnp.int32(0)
    for k in range(1, 4):
        delta = lax.bitwise_and(z - mates[k] - z0, 15)
        came = jnp.where(near_to(delta), k, came)
    part = piv.at[u, y, pl.ds(res_row, PIECE)]
    part[...] = mz[came]
    for dy, k in near:
        send(part, part, p_send.at[2], p_recv.at[2], at_tri(dy, window[k]))

    drain(a2r.at[0 : TRI - 1], a_recv)
    for g in range(GROUPS):
        gath0[g] = a2r[owner_ref[g * GROUPS]]
    for k in (3, 1, 2):
        send(gath0, gath[k], m_send, m_recv.at[k], at_tri(0, mates[k]))

    def row_of(place):
        return pl.multiple_of((lax.rem(place + 2 * NZ, NZ) // 4) * PIECE, PIECE)

    def hand_out(q):
        row = row_of(z - mates[q])
        for n, (dy, k) in enumerate(near):
            row_group, col_group, _ = groups_of(cells[dy, k])
            msg[q, n, 0] = gath[q][row_group]
            msg[q, n, 1] = gath[q][col_group]
            send(
                msg.at[q, n],
                fin.at[res, :, y, pl.ds(row, PIECE)],
                w_send,
                w_recv.at[q, k],
                at_tri(dy, window[k]),
            )
        row_group, col_group, _ = groups_of(cell)
        fin[res, 0, y, pl.ds(row, PIECE)] = gath[q][row_group]
        fin[res, 1, y, pl.ds(row, PIECE)] = gath[q][col_group]

    def part_of(q, k):
        source = z - window[k]
        b = lax.rem(source + NZ, 4)
        return b, row_of(source - mates[q])

    def over_x(q):
        for k in range(4):
            drain(msg.at[0, 0 : 3 if k == 0 else 4], w_recv.at[q, k])
            b, row = part_of(q, k)
            rows = pl.ds(row, PIECE)
            for n, dx in enumerate(others4):
                send(
                    fin.at[b, 1, :, rows],
                    right.at[u, b, :, rows],
                    x_send,
                    x_recv.at[q, n],
                    at_x(dx),
                )
            send(fin.at[b, 1, :, rows], right.at[u, b, :, rows], c_send, c_recv, sibling)

    def over_core(q):
        for n in (1, 2, 0):
            drain(right.at[0, :, :, 0:PIECE], x_recv.at[q, n])
            source = from_x(others4[n])
            for k in range(4):
                b, row = part_of(q, k)
                there = right.at[source, b, :, pl.ds(row, PIECE)]
                send(there, there, c_send, c_recv, sibling)

    hand_out(0)
    drain(wz.at[1:16], p_recv.at[2])
    strip = piv.at[u]
    for n, dx in enumerate(others4):
        send(strip, strip, p_send.at[3], q_recv.at[n], at_x(dx))
    send(strip, strip, q_send, p_recv.at[3], sibling)
    for q in (1, 2):
        drain(gath[q], m_recv.at[q])
        hand_out(q)
    over_x(0)
    for n in (1, 2, 0):
        drain(strip, q_recv.at[n])
        there = piv.at[from_x(others4[n])]
        send(there, there, q_send, p_recv.at[3], sibling)
    drain(gath[3], m_recv.at[3])
    hand_out(3)
    drain(piv.at[0:4], p_recv.at[3])
    whole_pivot(piv, p)
    keep_piv = pltpu.make_async_copy(piv, piv_out, k_sem.at[0])
    keep_piv.start()
    over_x(1)
    newton_start(p, xb, yv)
    over_x(2)
    newton_steps(p, xb, yv, 0, 1)
    over_core(0)
    newton_steps(p, xb, yv, 1, 2)
    over_x(3)
    for b in range(CB):
        right[u, b] = fin[b, 1]
    keep_fin = pltpu.make_async_copy(fin, fin_out, k_sem.at[1])
    keep_fin.start()
    newton_steps(p, xb, yv, 2, 4)
    over_core(1)
    over_core(2)
    newton_steps(p, xb, yv, 4, 5)
    over_core(3)

    yv[...] = jnp.where(identity(), 1.0, 0.0) - yv[...]
    size_ref[...] = jnp.broadcast_to(jnp.sum(yv[...] * yv[...]), size_ref.shape)
    xf[...] = xb[...].astype(F32)
    refine(xb, xl, xf, yv)
    scale_rows(fin, xb, xl, left)

    drain(right.at[0:4], c_recv)
    keep_right = pltpu.make_async_copy(right, right_out, k_sem.at[2])
    keep_right.start()
    products(left, right, rt, us)
    for slot in range(SLOTS):
        if slot not in LOAD_SLOTS:
            pltpu.make_async_copy(tiles_ref.at[0, slot], cur.at[slot], load_sem.at[slot]).wait()
        add_products(cell, us, cur, slot)
        pltpu.make_async_copy(cur.at[slot], upd.at[0, slot], o_sem.at[slot]).start()

    drain(wz.at[1:16], p_send.at[0])
    drain(mz.at[1:4], p_send.at[1])
    drain(wz.at[1:16], p_send.at[2])
    drain(piv.at[0:3], p_send.at[3])
    drain(piv.at[0:4], q_send)
    drain(a2r.at[0 : TRI - 1], a_send)
    drain(a2r.at[0 : 3 * GROUPS], m_send)
    drain(msg, w_send)
    drain(right.at[0:3], x_send)
    drain(right.at[0:4], c_send)
    keep_piv.wait()
    keep_fin.wait()
    keep_right.wait()
    for slot in range(SLOTS):
        pltpu.make_async_copy(cur.at[slot], upd.at[0, slot], o_sem.at[slot]).wait()


def result_kernel(
    size_ref,
    owner_any,
    tiles_ref,
    upd,
    fin_any,
    right_any,
    piv_any,
    out_ref,
    owner_ref,
    cur,
    fin,
    right,
    piv,
    p,
    xb,
    xl,
    xf,
    yv,
    left,
    rt,
    us,
    sem,
    out_sem,
):
    good = jnp.max(size_ref[...]) < SMALL

    @pl.when(good)
    def _():
        for slot in range(SLOTS):
            pltpu.make_async_copy(upd.at[0, slot], out_ref.at[0, slot], out_sem.at[slot]).start()
        for slot in range(SLOTS):
            pltpu.make_async_copy(upd.at[0, slot], out_ref.at[0, slot], out_sem.at[slot]).wait()

    @pl.when(jnp.logical_not(good))
    def _():
        pairs = (
            (owner_any, owner_ref),
            (tiles_ref.at[0], cur),
            (fin_any, fin),
            (right_any, right),
            (piv_any, piv),
        )
        for n, (src, dst) in enumerate(pairs):
            copy = pltpu.make_async_copy(src, dst, sem.at[n])
            copy.start()
            copy.wait()
        me = lax.axis_index("y") * NZ + lax.axis_index("z")
        (cell,) = cells_at(owner_ref, (me,))
        whole_pivot(piv, p)
        highest = lax.Precision.HIGHEST
        whole = p[...].astype(F32)
        rows = jnp.max(jnp.sum(jnp.abs(whole), axis=0, keepdims=True))
        xf[...] = whole * (-1.0 / rows) / rows

        def residual():
            yv[...] = jnp.where(identity(), 1.0, 0.0) - dot(p[...].astype(F32), xf[...], highest)
            return jnp.sum(yv[...] * yv[...])

        def more(carry):
            k, _ = carry
            xf[...] = xf[...] + dot(xf[...], yv[...], highest)
            return k + 1, residual()

        lax.while_loop(lambda s: (s[0] < 150) & (s[1] > 0.001), more, (0, residual()))
        refine(xb, xl, xf, yv)
        scale_rows(fin, xb, xl, left)
        products(left, right, rt, us)
        for slot in range(SLOTS):
            add_products(cell, us, cur, slot)
            copy = pltpu.make_async_copy(cur.at[slot], out_ref.at[0, slot], out_sem.at[slot])
            copy.start()
            copy.wait()


def shards(stored_tiles, cell_owner):
    dma = pltpu.SemaphoreType.DMA
    vmem = pl.BlockSpec(memory_space=pltpu.VMEM)
    anywhere = pl.BlockSpec(memory_space=pl.ANY)
    hbm = pl.BlockSpec(memory_space=pltpu.HBM)
    strip = (ROWS, LANES)
    fin_shape = (CB, 2, PER, *strip)
    right_shape = (SUB, CB, PER, *strip)
    piv_shape = (SUB, CB, *strip)
    work = [
        pltpu.VMEM((N, N), BF),
        pltpu.VMEM((N, N), BF),
        pltpu.VMEM((N, N), BF),
        pltpu.VMEM((N, N), F32),
        pltpu.VMEM((N, N), F32),
        pltpu.VMEM((PER * ROWS, N), BF),
        pltpu.VMEM((N, N), BF),
        pltpu.VMEM((PER, PER, ROWS, N), F32),
    ]
    owner = pltpu.SMEM((TRI,), jnp.int32)
    stored_tiles = pltpu.with_memory_space_constraint(stored_tiles, pltpu.HBM)
    cell_owner = pltpu.with_memory_space_constraint(cell_owner, pltpu.HBM)
    tiles = pltpu.VMEM((SLOTS, ROWS, N), F32)
    upd, size, fin, right, piv = pl.pallas_call(
        route_kernel,
        out_shape=(
            jax.ShapeDtypeStruct(stored_tiles.shape, F32),
            jax.ShapeDtypeStruct((8, LANES), F32),
            jax.ShapeDtypeStruct(fin_shape, BF),
            jax.ShapeDtypeStruct(right_shape, BF),
            jax.ShapeDtypeStruct(piv_shape, BF),
        ),
        in_specs=[pl.BlockSpec(memory_space=pltpu.SMEM), hbm],
        out_specs=(anywhere, vmem, hbm, hbm, hbm),
        scratch_shapes=[
            tiles,
            pltpu.VMEM((PER, CB, *strip), BF),
            pltpu.VMEM((TRI, PIECE, LANES), BF),
            pltpu.VMEM((GROUPS, PIECE, LANES), BF),
            pltpu.VMEM((GROUPS, PIECE, LANES), BF),
            pltpu.VMEM((GROUPS, PIECE, LANES), BF),
            pltpu.VMEM((GROUPS, PIECE, LANES), BF),
            pltpu.VMEM((4, 15, 2, PIECE, LANES), BF),
            pltpu.VMEM(fin_shape, BF),
            pltpu.VMEM(right_shape, BF),
            pltpu.VMEM(piv_shape, BF),
            pltpu.VMEM((16, PIECE, LANES), BF),
            pltpu.VMEM((4, PIECE, LANES), BF),
            *work,
            dma((SLOTS,)),
            dma((4,)),
            dma((4,)),
            dma,
            dma,
            dma,
            dma((4,)),
            dma,
            dma((4, 4)),
            dma,
            dma((4, 3)),
            dma,
            dma,
            dma,
            dma((3,)),
            dma((SLOTS,)),
            dma((3,)),
        ],
        compiler_params=pltpu.CompilerParams(
            collective_id=0, has_side_effects=True, vmem_limit_bytes=48 * 2**20
        ),
    )(cell_owner, stored_tiles)
    return pl.pallas_call(
        result_kernel,
        out_shape=jax.ShapeDtypeStruct(stored_tiles.shape, F32),
        in_specs=[vmem, anywhere, hbm, anywhere, hbm, hbm, hbm],
        out_specs=hbm,
        scratch_shapes=[
            owner,
            tiles,
            pltpu.VMEM(fin_shape, BF),
            pltpu.VMEM(right_shape, BF),
            pltpu.VMEM(piv_shape, BF),
            *work,
            dma((5,)),
            dma((SLOTS,)),
        ],
        compiler_params=pltpu.CompilerParams(vmem_limit_bytes=40 * 2**20),
    )(size, cell_owner, stored_tiles, upd, fin, right, piv)


def solution(mesh):
    torus = Mesh(mesh.devices.reshape(NY, NZ, NX, NC), AXES)
    spec = P(("y", "z"), None, ("x", "c"), None)
    return jax.shard_map(
        shards, mesh=torus, in_specs=(spec, P()), out_specs=spec, check_vma=False
    )
```
